32 devices in a mesh: slab: 8 (over z, y), leaf: 4 (over x, core).
Axes of the slice: x: 2, y: 2, z: 4, core: 2. Of those that a mesh axis runs over, the one named last changes fastest.
Arguments:
- probes: bfloat16 [16384, 128], P(('slab', 'leaf')), may hold values from -6 to 6
- near_blocks: bfloat16 [32, 3, 512, 512], P(('slab', 'leaf')), may hold values from -0.15625 to 0.15625
- near_offsets: int32 [32, 3], P(('slab', 'leaf')), may hold values from -1 to 1
- far_basis: bfloat16 [5, 16384, 128], P(None, ('slab', 'leaf')), may hold values from -0.25 to 0.25
Outputs:
- product: float32 [16384, 128], P(('slab', 'leaf'))
The draws below stay inside these ranges and needn't reach their ends.
Inputs may be any that keep to these rules, and one draw needn't show every extreme that they name: `near_offsets`: offsets that point outside the leaves meet zero probes.
All inputs are finite; a program needn't handle non-finite values.
Results may differ from the reference program's by a relative error of at most 0.0025.
Values may be sent and summed in bfloat16 or wider, within the bound.
A program may use at most 64 MiB of HBM per device.

```python
import jax
import jax.numpy as jnp
from jax import lax

POINTS_LEAF = 512
RANK = 128
NEAR = 3
PROBES = 128
LEAVES = 32
POINTS = 16384
LEVELS = 5


def place_ends(entries, rng, low, high):
    longest = entries.shape.index(max(entries.shape))
    spots = []
    for shift in (0, 1):
        where = [jax.random.randint(jax.random.fold_in(rng, axis), (), 0, length) for axis, length in enumerate(entries.shape)]
        where[longest] = (where[longest] + shift) % entries.shape[longest]
        spots.append(tuple(where))
    return entries.at[spots[0]].set(low).at[spots[1]].set(high)


def block_levels(key, extent, pieces, smallest, top_value):
    gain, own = 1.0, jax.random.fold_in(key, 6)
    for axis_at, shards_of in pieces:
        draws = jnp.exp(jax.random.uniform(jax.random.fold_in(own, axis_at), (shards_of,), jnp.float32, smallest / len(pieces), top_value / len(pieces)))
        gain = gain * jnp.repeat(draws, extent[axis_at] // shards_of).reshape([-1 if axis == axis_at else 1 for axis in range(len(extent))])
    return gain


def noise(own_key, dims, scale, most, shards=(), kind=jnp.bfloat16):
    array = scale * jax.random.normal(own_key, dims, jnp.float32)
    if shards:
        array = array * block_levels(own_key, dims, shards, -0.22, 0.18)
    return jnp.clip(array, -most, most).astype(kind)


def setup_inputs(seed: int = 0) -> dict:
    keys = jax.random.split(jax.random.key(seed), 5)
    probes = noise(keys[0], (POINTS, PROBES), 1.0, 6.0, ((0, 32),))
    near_blocks = noise(keys[1], (LEAVES, NEAR, POINTS_LEAF, POINTS_LEAF), (NEAR * POINTS_LEAF) ** -0.5, 0.15625, ((0, 32),))
    near_offsets = place_ends(jax.random.randint(keys[2], (LEAVES, NEAR), -1, 2), jax.random.fold_in(keys[2], 1), -1, 1).astype(jnp.int32)
    far_basis = noise(keys[3], (LEVELS, POINTS, RANK), POINTS_LEAF ** -0.5, 0.25, ((1, 32),))
    return {"probes": probes, "near_blocks": near_blocks, "near_offsets": near_offsets, "far_basis": far_basis}


def reference(probes, near_blocks, near_offsets, far_basis):
    leaves = near_blocks.shape[0]
    blocks = probes.reshape(leaves, POINTS_LEAF, PROBES)
    empty = jnp.zeros((1, POINTS_LEAF, PROBES), probes.dtype)
    padded = jnp.concatenate([empty, blocks, empty], axis=0)

    def near_leaf(packed_args):
        block_set, offset_row, leaf_index = packed_args
        near_sum = jnp.zeros((POINTS_LEAF, PROBES), jnp.float32)
        for member in range(NEAR):
            where_from = (leaf_index + offset_row[member] + 1).astype(jnp.int32)
            neighbour = lax.dynamic_index_in_dim(padded, where_from, 0, keepdims=False)
            near_sum = near_sum + jnp.dot(block_set[member], neighbour, preferred_element_type=jnp.float32)
        return near_sum

    output = lax.map(near_leaf, (near_blocks, near_offsets, jnp.arange(leaves, dtype=jnp.int32)))
    wide_probes = blocks.astype(jnp.float32)
    for level in range(LEVELS):
        level_basis = far_basis[level].reshape(leaves, POINTS_LEAF, RANK).astype(jnp.float32)
        projected = jnp.einsum("npr,npq->nrq", level_basis, wide_probes)
        nodes = leaves >> (level + 1)
        grouped = projected.reshape(nodes, 2, 2 ** level, RANK, PROBES).sum(axis=2)
        swapped = grouped[:, ::-1]
        sibling = jnp.broadcast_to(swapped[:, :, None], (nodes, 2, 2 ** level, RANK, PROBES)).reshape(leaves, RANK, PROBES)
        coupling = (sibling * (2.0 ** (-0.5 * level))).astype(jnp.bfloat16)
        output = output + jnp.einsum("npr,nrq->npq", level_basis, coupling.astype(jnp.float32))
    return output.reshape(leaves * POINTS_LEAF, PROBES)
```

```python
import functools

import jax
import jax.numpy as jnp
from jax import lax
from jax.experimental import pallas as pl
from jax.experimental.pallas import tpu as pltpu
from jax.sharding import PartitionSpec as P

MESH = pl.DeviceIdType.MESH
DIRECT_LEVELS = 5


def flipped(index, mask):
    bit = 1
    result = index
    while bit <= mask:
        if mask & bit:
            result = result + bit * (1 - 2 * ((index // bit) % 2))
        bit *= 2
    return result


def owner_parity(level):
    return None if level < 3 else level % 2


def owner_count(level):
    return 2**level if level < 3 else 2 ** (level - 1)


def kernel(
    levels, slabs, leaves, offsets, probes_hbm, near_hbm, far_hbm, out_hbm,
    window, near, far, partial, arrived, piece, coupling, out,
    load_sem, out_sem, sum_send, sum_recv, piece_send, piece_recv, probe_send, probe_recv,
):
    slab, leaf = lax.axis_index("slab"), lax.axis_index("leaf")
    me = slab * leaves + leaf
    core = leaf % 2
    total = slabs * leaves
    group = 2**levels
    rank = partial.shape[1]
    points = window.shape[1]

    def device(mask):
        return flipped(slab, mask // leaves), flipped(leaf, mask % leaves)

    def along(step):
        other = me + step
        return other // leaves, other % leaves

    load_probes = pltpu.make_async_copy(probes_hbm, window.at[1], load_sem.at[0])
    load_far = pltpu.make_async_copy(far_hbm.at[pl.ds(0, levels)], far, load_sem.at[1])
    load_near = pltpu.make_async_copy(near_hbm.at[0], near, load_sem.at[2])
    load_probes.start()
    load_far.start()
    load_near.start()

    has_low, has_high = me > 0, me < total - 1
    barrier = pltpu.get_barrier_semaphore()
    for mask in range(1, group):
        pl.semaphore_signal(barrier, inc=1, device_id=device(mask), device_id_type=MESH)
    if total > group:
        low_outside = jnp.logical_and(has_low, me % group == 0)
        high_outside = jnp.logical_and(has_high, me % group == group - 1)
        for outside, step in ((low_outside, -1), (high_outside, 1)):
            @pl.when(outside)
            def _():
                pl.semaphore_signal(barrier, inc=1, device_id=along(step), device_id_type=MESH)

    load_probes.wait()
    load_far.wait()
    turned = window[1].T
    for level in reversed(range(levels)):
        partial[level] = jnp.dot(turned, far[level], preferred_element_type=jnp.float32)
    piece[0] = partial[0].astype(jnp.bfloat16)

    pl.semaphore_wait(barrier, group - 1)
    if total > group:
        for outside in (low_outside, high_outside):
            @pl.when(outside)
            def _():
                pl.semaphore_wait(barrier, 1)

    def remote(source, target, send, recv, where):
        return pltpu.make_async_remote_copy(
            src_ref=source, dst_ref=target, send_sem=send, recv_sem=recv,
            device_id=where, device_id_type=MESH,
        )

    def rows_of(level, index):
        count = owner_count(level)
        chunk = index % 2**level
        if owner_parity(level) is not None:
            chunk = chunk // 2
        height = rank // count
        return pl.ds(pl.multiple_of(chunk * height, height), height)

    for level in reversed(range(1, levels)):
        parity = owner_parity(level)
        if parity is None:
            for mask in range(1, 2**level):
                where = device(mask)
                remote(
                    partial.at[level, rows_of(level, flipped(me, mask))],
                    arrived[level - 1].at[mask],
                    sum_send.at[level], sum_recv.at[level], where,
                ).start()
        else:
            differs = (core + parity) % 2
            for pair in reversed(range(2 ** (level - 1))):
                where_slab, where_leaf = device(2 * pair)
                where = where_slab, where_leaf - core + parity
                index = where[0] * leaves + where[1]

                def send():
                    remote(
                        partial.at[level, rows_of(level, index)],
                        arrived[level - 1].at[2 * pair + differs],
                        sum_send.at[level], sum_recv.at[level], where,
                    ).start()

                if pair == 0:
                    pl.when(differs == 1)(send)
                else:
                    send()

    remote(piece.at[0], coupling.at[0], piece_send.at[0], piece_recv.at[0], device(1)).start()

    to_low = remote(window.at[1], window.at[2], probe_send.at[0], probe_recv.at[1], along(-1))
    to_high = remote(window.at[1], window.at[0], probe_send.at[1], probe_recv.at[0], along(1))
    pl.when(has_low)(to_low.start)
    pl.when(has_high)(to_high.start)

    def await_bytes(ref, sem):
        pltpu.make_async_copy(ref, ref, sem).wait()

    def finish(level):
        rows = rows_of(level, me)
        height = rank // owner_count(level)
        members = 2**level
        await_bytes(arrived[level - 1].at[pl.ds(1, members - 1)], sum_recv.at[level])
        value = partial[level, rows]
        for member in range(1, members):
            value = value + arrived[level - 1][member]
        value = (value * 2.0 ** (-0.5 * level)).astype(jnp.bfloat16)
        piece[level, pl.ds(0, height)] = value
        for mask in reversed(range(members, 2 * members)):
            remote(
                piece.at[level, pl.ds(0, height)], coupling.at[level, rows],
                piece_send.at[level], piece_recv.at[level], device(mask),
            ).start()

    for level in reversed(range(1, levels)):
        parity = owner_parity(level)
        if parity is None:
            finish(level)
        else:
            pl.when(core == parity)(functools.partial(finish, level))

    @pl.when(jnp.logical_not(has_low))
    def _():
        window[0] = jnp.zeros_like(window[0])

    @pl.when(jnp.logical_not(has_high))
    def _():
        window[2] = jnp.zeros_like(window[2])

    pl.when(has_high)(lambda: await_bytes(window.at[2], probe_recv.at[1]))
    pl.when(has_low)(lambda: await_bytes(window.at[0], probe_recv.at[0]))
    load_near.wait()
    members = near.shape[0]
    value = jnp.dot(near[0], window[offsets[0, 0] + 1], preferred_element_type=jnp.float32)
    for member in range(1, members):
        value = value + jnp.dot(
            near[member], window[offsets[0, member] + 1], preferred_element_type=jnp.float32
        )
    out[...] = value

    for level in range(levels):
        await_bytes(coupling.at[level], piece_recv.at[level])
    value = out[...]
    for level in range(levels):
        value = value + lax.dot_general(
            far[level], coupling[level], (((1,), (1,)), ((), ())),
            preferred_element_type=jnp.float32,
        )
    out[...] = value
    store = pltpu.make_async_copy(out, out_hbm, out_sem)
    store.start()

    await_bytes(piece.at[0], piece_send.at[0])
    for level in range(1, levels):
        parity = owner_parity(level)
        height = rank // owner_count(level)
        if parity is None:
            await_bytes(partial.at[level, pl.ds(0, rank - height)], sum_send.at[level])
            await_bytes(coupling.at[level], piece_send.at[level])
        else:
            @pl.when(core == parity)
            def _():
                await_bytes(partial.at[level, pl.ds(0, rank - height)], sum_send.at[level])
                await_bytes(coupling.at[pl.ds(0, 2)], piece_send.at[level])

            @pl.when(core != parity)
            def _():
                await_bytes(partial.at[level], sum_send.at[level])

    pl.when(has_low)(to_low.wait_send)
    pl.when(has_high)(to_high.wait_send)
    store.wait()


def direct(probes, near_blocks, near_offsets, far_basis, levels):
    points, columns = probes.shape
    rank = far_basis.shape[2]
    members = near_blocks.shape[1]
    slabs, leaves = lax.axis_size("slab"), lax.axis_size("leaf")
    arrived = [
        pltpu.VMEM((2**level, rank // owner_count(level), columns), jnp.float32)
        for level in range(1, levels)
    ]
    flops = 2 * points * columns * (members * points + 2 * levels * rank)
    return pl.pallas_call(
        functools.partial(kernel, levels, slabs, leaves),
        out_shape=jax.ShapeDtypeStruct((points, columns), jnp.float32),
        in_specs=[pl.BlockSpec(memory_space=pltpu.SMEM)] + [pl.BlockSpec(memory_space=pl.ANY)] * 3,
        out_specs=pl.BlockSpec(memory_space=pl.ANY),
        scratch_shapes=[
            pltpu.VMEM((3, points, columns), jnp.bfloat16),
            pltpu.VMEM((members, points, points), jnp.bfloat16),
            pltpu.VMEM((levels, points, rank), jnp.bfloat16),
            pltpu.VMEM((levels, columns, rank), jnp.float32),
            arrived,
            pltpu.VMEM((levels, columns, rank), jnp.bfloat16),
            pltpu.VMEM((levels, columns, rank), jnp.bfloat16),
            pltpu.VMEM((points, columns), jnp.float32),
            pltpu.SemaphoreType.DMA((3,)),
            pltpu.SemaphoreType.DMA,
            pltpu.SemaphoreType.DMA((levels,)),
            pltpu.SemaphoreType.DMA((levels,)),
            pltpu.SemaphoreType.DMA((levels,)),
            pltpu.SemaphoreType.DMA((levels,)),
            pltpu.SemaphoreType.DMA((2,)),
            pltpu.SemaphoreType.DMA((2,)),
        ],
        compiler_params=pltpu.CompilerParams(
            collective_id=0, has_side_effects=True, vmem_limit_bytes=24 * 2**20
        ),
        cost_estimate=pl.CostEstimate(flops=flops, bytes_accessed=2 * near_blocks.size, transcendentals=0),
    )(near_offsets, probes, near_blocks, far_basis)


def swapped(value, axis, bit):
    mask = 2**bit
    pairs = [(source, source ^ mask) for source in range(lax.axis_size(axis))]
    return lax.ppermute(value, axis, pairs)


def upper(output, probes, far_basis, first):
    levels = far_basis.shape[0]
    partial_sums = {
        level: lax.dot_general(
            far_basis[level], probes, (((0,), (0,)), ((), ())), preferred_element_type=jnp.float32
        )
        for level in range(first, levels)
    }
    leaf_bits = lax.axis_size("leaf").bit_length() - 1
    for bit in range(levels):
        axis, axis_bit = ("leaf", bit) if bit < leaf_bits else ("slab", bit - leaf_bits)
        kept = [level for level in range(first, levels) if level >= bit]
        incoming = swapped(jnp.stack([partial_sums[level] for level in kept]), axis, axis_bit)
        for place, level in enumerate(kept):
            if level == bit:
                coupling = (incoming[place] * 2.0 ** (-0.5 * level)).astype(jnp.bfloat16)
                output = output + jnp.dot(
                    far_basis[level], coupling, preferred_element_type=jnp.float32
                )
            else:
                partial_sums[level] = partial_sums[level] + incoming[place]
    return output


def body(probes, near_blocks, near_offsets, far_basis):
    levels = far_basis.shape[0]
    first = min(levels, DIRECT_LEVELS)
    output = direct(probes, near_blocks, near_offsets, far_basis, first)
    if levels > first:
        output = upper(output, probes, far_basis, first)
    return output


def solution(mesh):
    return jax.shard_map(
        body,
        mesh=mesh,
        in_specs=(
            P(("slab", "leaf"), None),
            P(("slab", "leaf"), None, None, None),
            P(("slab", "leaf"), None),
            P(None, ("slab", "leaf"), None),
        ),
        out_specs=P(("slab", "leaf"), None),
        check_vma=False,
    )
```

```python
import functools

import jax
import jax.numpy as jnp
from jax import lax
from jax.experimental import pallas as pl
from jax.experimental.pallas import tpu as pltpu
from jax.sharding import PartitionSpec as P

MESH = pl.DeviceIdType.MESH
DIRECT_LEVELS = 5


def flipped(index, mask):
    bit = 1
    result = index
    while bit <= mask:
        if mask & bit:
            result = result + bit * (1 - 2 * ((index // bit) % 2))
        bit *= 2
    return result


def owner_parity(level):
    return None if level < 3 else level % 2


def owner_count(level):
    return 2**level if level < 3 else 2 ** (level - 1)


def kernel(
    levels, slabs, leaves, offsets_hbm, probes_hbm, near_hbm, far_hbm, out_hbm,
    offsets, window, near, far, partial, arrived, piece, coupling, out,
    load_sem, out_sem, sum_send, sum_recv, piece_send, piece_recv, probe_send, probe_recv,
):
    slab, leaf = lax.axis_index("slab"), lax.axis_index("leaf")
    me = slab * leaves + leaf
    core = leaf % 2
    total = slabs * leaves
    group = 2**levels
    rank = partial.shape[1]
    points = window.shape[1]

    def device(mask):
        return flipped(slab, mask // leaves), flipped(leaf, mask % leaves)

    def along(step):
        other = me + step
        return other // leaves, other % leaves

    load_probes = pltpu.make_async_copy(probes_hbm, window.at[1], load_sem.at[0])
    load_far = pltpu.make_async_copy(far_hbm.at[pl.ds(0, levels)], far, load_sem.at[1])
    load_near = pltpu.make_async_copy(near_hbm.at[0], near, load_sem.at[2])
    load_offsets = pltpu.make_async_copy(offsets_hbm, offsets, load_sem.at[3])
    load_probes.start()
    load_far.start()
    load_offsets.start()
    load_near.start()

    has_low, has_high = me > 0, me < total - 1
    barrier = pltpu.get_barrier_semaphore()
    for mask in range(1, group):
        pl.semaphore_signal(barrier, inc=1, device_id=device(mask), device_id_type=MESH)
    if total > group:
        low_outside = jnp.logical_and(has_low, me % group == 0)
        high_outside = jnp.logical_and(has_high, me % group == group - 1)
        for outside, step in ((low_outside, -1), (high_outside, 1)):
            @pl.when(outside)
            def _():
                pl.semaphore_signal(barrier, inc=1, device_id=along(step), device_id_type=MESH)

    load_probes.wait()
    load_far.wait()
    turned = window[1].T
    for level in reversed(range(levels)):
        partial[level] = jnp.dot(turned, far[level], preferred_element_type=jnp.float32)
    piece[0] = partial[0].astype(jnp.bfloat16)

    pl.semaphore_wait(barrier, group - 1)
    if total > group:
        for outside in (low_outside, high_outside):
            @pl.when(outside)
            def _():
                pl.semaphore_wait(barrier, 1)

    def remote(source, target, send, recv, where):
        return pltpu.make_async_remote_copy(
            src_ref=source, dst_ref=target, send_sem=send, recv_sem=recv,
            device_id=where, device_id_type=MESH,
        )

    def rows_of(level, index):
        count = owner_count(level)
        chunk = index % 2**level
        if owner_parity(level) is not None:
            chunk = chunk // 2
        height = rank // count
        return pl.ds(pl.multiple_of(chunk * height, height), height)

    for level in reversed(range(1, levels)):
        parity = owner_parity(level)
        if parity is None:
            for mask in range(1, 2**level):
                where = device(mask)
                remote(
                    partial.at[level, rows_of(level, flipped(me, mask))],
                    arrived[level - 1].at[mask],
                    sum_send.at[level], sum_recv.at[level], where,
                ).start()
        else:
            differs = (core + parity) % 2
            for pair in reversed(range(2 ** (level - 1))):
                where_slab, where_leaf = device(2 * pair)
                where = where_slab, where_leaf - core + parity
                index = where[0] * leaves + where[1]

                def send():
                    remote(
                        partial.at[level, rows_of(level, index)],
                        arrived[level - 1].at[2 * pair + differs],
                        sum_send.at[level], sum_recv.at[level], where,
                    ).start()

                if pair == 0:
                    pl.when(differs == 1)(send)
                else:
                    send()

    remote(piece.at[0], coupling.at[0], piece_send.at[0], piece_recv.at[0], device(1)).start()

    to_low = remote(window.at[1], window.at[2], probe_send.at[0], probe_recv.at[1], along(-1))
    to_high = remote(window.at[1], window.at[0], probe_send.at[1], probe_recv.at[0], along(1))
    pl.when(has_low)(to_low.start)
    pl.when(has_high)(to_high.start)

    def await_bytes(ref, sem):
        pltpu.make_async_copy(ref, ref, sem).wait()

    def finish(level):
        rows = rows_of(level, me)
        height = rank // owner_count(level)
        members = 2**level
        await_bytes(arrived[level - 1].at[pl.ds(1, members - 1)], sum_recv.at[level])
        value = partial[level, rows]
        for member in range(1, members):
            value = value + arrived[level - 1][member]
        value = (value * 2.0 ** (-0.5 * level)).astype(jnp.bfloat16)
        piece[level, pl.ds(0, height)] = value
        for mask in reversed(range(members, 2 * members)):
            remote(
                piece.at[level, pl.ds(0, height)], coupling.at[level, rows],
                piece_send.at[level], piece_recv.at[level], device(mask),
            ).start()

    for level in reversed(range(1, levels)):
        parity = owner_parity(level)
        if parity is None:
            finish(level)
        else:
            pl.when(core == parity)(functools.partial(finish, level))

    @pl.when(jnp.logical_not(has_low))
    def _():
        window[0] = jnp.zeros_like(window[0])

    @pl.when(jnp.logical_not(has_high))
    def _():
        window[2] = jnp.zeros_like(window[2])

    pl.when(has_high)(lambda: await_bytes(window.at[2], probe_recv.at[1]))
    pl.when(has_low)(lambda: await_bytes(window.at[0], probe_recv.at[0]))
    load_near.wait()
    load_offsets.wait()
    members = near.shape[0]
    value = jnp.dot(near[0], window[offsets[0, 0] + 1], preferred_element_type=jnp.float32)
    for member in range(1, members):
        value = value + jnp.dot(
            near[member], window[offsets[0, member] + 1], preferred_element_type=jnp.float32
        )
    out[...] = value

    for level in range(levels):
        await_bytes(coupling.at[level], piece_recv.at[level])
    value = out[...]
    for level in range(levels):
        value = value + lax.dot_general(
            far[level], coupling[level], (((1,), (1,)), ((), ())),
            preferred_element_type=jnp.float32,
        )
    out[...] = value
    store = pltpu.make_async_copy(out, out_hbm, out_sem)
    store.start()

    await_bytes(piece.at[0], piece_send.at[0])
    for level in range(1, levels):
        parity = owner_parity(level)
        height = rank // owner_count(level)
        if parity is None:
            await_bytes(partial.at[level, pl.ds(0, rank - height)], sum_send.at[level])
            await_bytes(coupling.at[level], piece_send.at[level])
        else:
            @pl.when(core == parity)
            def _():
                await_bytes(partial.at[level, pl.ds(0, rank - height)], sum_send.at[level])
                await_bytes(coupling.at[pl.ds(0, 2)], piece_send.at[level])

            @pl.when(core != parity)
            def _():
                await_bytes(partial.at[level], sum_send.at[level])

    pl.when(has_low)(to_low.wait_send)
    pl.when(has_high)(to_high.wait_send)
    store.wait()


def direct(probes, near_blocks, near_offsets, far_basis, levels):
    points, columns = probes.shape
    rank = far_basis.shape[2]
    members = near_blocks.shape[1]
    slabs, leaves = lax.axis_size("slab"), lax.axis_size("leaf")
    arrived = [
        pltpu.VMEM((2**level, rank // owner_count(level), columns), jnp.float32)
        for level in range(1, levels)
    ]
    flops = 2 * points * columns * (members * points + 2 * levels * rank)
    return pl.pallas_call(
        functools.partial(kernel, levels, slabs, leaves),
        out_shape=jax.ShapeDtypeStruct((points, columns), jnp.float32),
        in_specs=[pl.BlockSpec(memory_space=pl.ANY)] * 4,
        out_specs=pl.BlockSpec(memory_space=pl.ANY),
        scratch_shapes=[
            pltpu.SMEM((1, members), jnp.int32),
            pltpu.VMEM((3, points, columns), jnp.bfloat16),
            pltpu.VMEM((members, points, points), jnp.bfloat16),
            pltpu.VMEM((levels, points, rank), jnp.bfloat16),
            pltpu.VMEM((levels, columns, rank), jnp.float32),
            arrived,
            pltpu.VMEM((levels, columns, rank), jnp.bfloat16),
            pltpu.VMEM((levels, columns, rank), jnp.bfloat16),
            pltpu.VMEM((points, columns), jnp.float32),
            pltpu.SemaphoreType.DMA((4,)),
            pltpu.SemaphoreType.DMA,
            pltpu.SemaphoreType.DMA((levels,)),
            pltpu.SemaphoreType.DMA((levels,)),
            pltpu.SemaphoreType.DMA((levels,)),
            pltpu.SemaphoreType.DMA((levels,)),
            pltpu.SemaphoreType.DMA((2,)),
            pltpu.SemaphoreType.DMA((2,)),
        ],
        compiler_params=pltpu.CompilerParams(
            collective_id=0, has_side_effects=True, vmem_limit_bytes=60 * 2**20
        ),
        cost_estimate=pl.CostEstimate(flops=flops, bytes_accessed=2 * near_blocks.size, transcendentals=0),
    )(near_offsets, probes, near_blocks, far_basis)


def swapped(value, axis, bit):
    mask = 2**bit
    pairs = [(source, source ^ mask) for source in range(lax.axis_size(axis))]
    return lax.ppermute(value, axis, pairs)


def upper(output, probes, far_basis, first):
    levels = far_basis.shape[0]
    partial_sums = {
        level: lax.dot_general(
            far_basis[level], probes, (((0,), (0,)), ((), ())), preferred_element_type=jnp.float32
        )
        for level in range(first, levels)
    }
    leaf_bits = lax.axis_size("leaf").bit_length() - 1
    for bit in range(levels):
        axis, axis_bit = ("leaf", bit) if bit < leaf_bits else ("slab", bit - leaf_bits)
        kept = [level for level in range(first, levels) if level >= bit]
        incoming = swapped(jnp.stack([partial_sums[level] for level in kept]), axis, axis_bit)
        for place, level in enumerate(kept):
            if level == bit:
                coupling = (incoming[place] * 2.0 ** (-0.5 * level)).astype(jnp.bfloat16)
                output = output + jnp.dot(
                    far_basis[level], coupling, preferred_element_type=jnp.float32
                )
            else:
                partial_sums[level] = partial_sums[level] + incoming[place]
    return output


def body(probes, near_blocks, near_offsets, far_basis):
    levels = far_basis.shape[0]
    first = min(levels, DIRECT_LEVELS)
    output = direct(probes, near_blocks, near_offsets, far_basis, first)
    if levels > first:
        output = upper(output, probes, far_basis, first)
    return output


def solution(mesh):
    return jax.shard_map(
        body,
        mesh=mesh,
        in_specs=(
            P(("slab", "leaf"), None),
            P(("slab", "leaf"), None, None, None),
            P(("slab", "leaf"), None),
            P(None, ("slab", "leaf"), None),
        ),
        out_specs=P(("slab", "leaf"), None),
        check_vma=False,
    )
```

```python
import functools

import jax
import jax.numpy as jnp
from jax import lax
from jax.experimental import pallas as pl
from jax.experimental.pallas import tpu as pltpu
from jax.sharding import PartitionSpec as P

MESH = pl.DeviceIdType.MESH
DIRECT_LEVELS = 5


def flipped(index, mask):
    bit = 1
    result = index
    while bit <= mask:
        if mask & bit:
            result = result + bit * (1 - 2 * ((index // bit) % 2))
        bit *= 2
    return result


def owner_parity(level):
    return None if level < 3 else level % 2


def owner_count(level):
    return 2**level if level < 3 else 2 ** (level - 1)


def kernel(
    levels, slabs, leaves, offsets_hbm, probes_hbm, near_hbm, far_hbm, out_hbm, coupling,
    offsets, window, near, far, partial, arrived, piece, out,
    load_sem, out_sem, sum_send, sum_recv, piece_send, piece_recv, probe_send, probe_recv,
):
    slab, leaf = lax.axis_index("slab"), lax.axis_index("leaf")
    me = slab * leaves + leaf
    core = leaf % 2
    total = slabs * leaves
    group = 2**levels
    rank = partial.shape[1]
    points = window.shape[1]

    def device(mask):
        return flipped(slab, mask // leaves), flipped(leaf, mask % leaves)

    def along(step):
        other = me + step
        return other // leaves, other % leaves

    load_probes = pltpu.make_async_copy(probes_hbm, window.at[1], load_sem.at[0])
    load_far = pltpu.make_async_copy(far_hbm.at[pl.ds(0, levels)], far, load_sem.at[1])
    load_near = pltpu.make_async_copy(near_hbm.at[0], near, load_sem.at[2])
    load_offsets = pltpu.make_async_copy(offsets_hbm, offsets, load_sem.at[3])
    load_probes.start()
    load_far.start()
    load_offsets.start()
    load_near.start()

    has_low, has_high = me > 0, me < total - 1
    barrier = pltpu.get_barrier_semaphore()
    for mask in range(1, group):
        pl.semaphore_signal(barrier, inc=1, device_id=device(mask), device_id_type=MESH)
    if total > group:
        low_outside = jnp.logical_and(has_low, me % group == 0)
        high_outside = jnp.logical_and(has_high, me % group == group - 1)
        for outside, step in ((low_outside, -1), (high_outside, 1)):
            @pl.when(outside)
            def _():
                pl.semaphore_signal(barrier, inc=1, device_id=along(step), device_id_type=MESH)

    load_probes.wait()
    load_far.wait()
    turned = window[1].T
    for level in reversed(range(levels)):
        partial[level] = jnp.dot(turned, far[level], preferred_element_type=jnp.float32)
    piece[0] = partial[0].astype(jnp.bfloat16)

    pl.semaphore_wait(barrier, group - 1)
    if total > group:
        for outside in (low_outside, high_outside):
            @pl.when(outside)
            def _():
                pl.semaphore_wait(barrier, 1)

    def remote(source, target, send, recv, where):
        return pltpu.make_async_remote_copy(
            src_ref=source, dst_ref=target, send_sem=send, recv_sem=recv,
            device_id=where, device_id_type=MESH,
        )

    def rows_of(level, index):
        count = owner_count(level)
        chunk = index % 2**level
        if owner_parity(level) is not None:
            chunk = chunk // 2
        height = rank // count
        return pl.ds(pl.multiple_of(chunk * height, height), height)

    for level in reversed(range(1, levels)):
        parity = owner_parity(level)
        if parity is None:
            for mask in range(1, 2**level):
                where = device(mask)
                remote(
                    partial.at[level, rows_of(level, flipped(me, mask))],
                    arrived[level - 1].at[mask],
                    sum_send.at[level], sum_recv.at[level], where,
                ).start()
        else:
            differs = (core + parity) % 2
            for pair in reversed(range(2 ** (level - 1))):
                where_slab, where_leaf = device(2 * pair)
                where = where_slab, where_leaf - core + parity
                index = where[0] * leaves + where[1]

                def send():
                    remote(
                        partial.at[level, rows_of(level, index)],
                        arrived[level - 1].at[2 * pair + differs],
                        sum_send.at[level], sum_recv.at[level], where,
                    ).start()

                if pair == 0:
                    pl.when(differs == 1)(send)
                else:
                    send()

    remote(piece.at[0], coupling.at[0], piece_send.at[0], piece_recv.at[0], device(1)).start()

    to_low = remote(window.at[1], window.at[2], probe_send.at[0], probe_recv.at[1], along(-1))
    to_high = remote(window.at[1], window.at[0], probe_send.at[1], probe_recv.at[0], along(1))
    pl.when(has_low)(to_low.start)
    pl.when(has_high)(to_high.start)

    def await_bytes(ref, sem):
        pltpu.make_async_copy(ref, ref, sem).wait()

    def finish(level):
        rows = rows_of(level, me)
        height = rank // owner_count(level)
        members = 2**level
        await_bytes(arrived[level - 1].at[pl.ds(1, members - 1)], sum_recv.at[level])
        value = partial[level, rows]
        for member in range(1, members):
            value = value + arrived[level - 1][member]
        value = (value * 2.0 ** (-0.5 * level)).astype(jnp.bfloat16)
        piece[level, pl.ds(0, height)] = value
        for mask in reversed(range(members, 2 * members)):
            remote(
                piece.at[level, pl.ds(0, height)], coupling.at[level, rows],
                piece_send.at[level], piece_recv.at[level], device(mask),
            ).start()

    for level in reversed(range(1, levels)):
        parity = owner_parity(level)
        if parity is None:
            finish(level)
        else:
            pl.when(core == parity)(functools.partial(finish, level))

    @pl.when(jnp.logical_not(has_low))
    def _():
        window[0] = jnp.zeros_like(window[0])

    @pl.when(jnp.logical_not(has_high))
    def _():
        window[2] = jnp.zeros_like(window[2])

    pl.when(has_high)(lambda: await_bytes(window.at[2], probe_recv.at[1]))
    pl.when(has_low)(lambda: await_bytes(window.at[0], probe_recv.at[0]))
    load_near.wait()
    load_offsets.wait()
    members = near.shape[0]
    value = jnp.dot(near[0], window[offsets[0, 0] + 1], preferred_element_type=jnp.float32)
    for member in range(1, members):
        value = value + jnp.dot(
            near[member], window[offsets[0, member] + 1], preferred_element_type=jnp.float32
        )
    out[...] = value

    store = pltpu.make_async_copy(out, out_hbm, out_sem)
    store.start()
    for level in range(levels):
        await_bytes(coupling.at[level], piece_recv.at[level])

    await_bytes(piece.at[0], piece_send.at[0])
    for level in range(1, levels):
        parity = owner_parity(level)
        height = rank // owner_count(level)
        if parity is None:
            await_bytes(partial.at[level, pl.ds(0, rank - height)], sum_send.at[level])
            await_bytes(coupling.at[level], piece_send.at[level])
        else:
            @pl.when(core == parity)
            def _():
                await_bytes(partial.at[level, pl.ds(0, rank - height)], sum_send.at[level])
                await_bytes(coupling.at[pl.ds(0, 2)], piece_send.at[level])

            @pl.when(core != parity)
            def _():
                await_bytes(partial.at[level], sum_send.at[level])

    pl.when(has_low)(to_low.wait_send)
    pl.when(has_high)(to_high.wait_send)
    store.wait()


def direct(probes, near_blocks, near_offsets, far_basis, levels):
    points, columns = probes.shape
    rank = far_basis.shape[2]
    members = near_blocks.shape[1]
    slabs, leaves = lax.axis_size("slab"), lax.axis_size("leaf")
    arrived = [
        pltpu.VMEM((2**level, rank // owner_count(level), columns), jnp.float32)
        for level in range(1, levels)
    ]
    flops = 2 * points * columns * (members * points + 2 * levels * rank)
    return pl.pallas_call(
        functools.partial(kernel, levels, slabs, leaves),
        out_shape=[
            jax.ShapeDtypeStruct((points, columns), jnp.float32),
            jax.ShapeDtypeStruct((levels, columns, rank), jnp.bfloat16),
        ],
        in_specs=[pl.BlockSpec(memory_space=pl.ANY)] * 4,
        out_specs=[pl.BlockSpec(memory_space=pl.ANY)] * 2,
        scratch_shapes=[
            pltpu.SMEM((1, members), jnp.int32),
            pltpu.VMEM((3, points, columns), jnp.bfloat16),
            pltpu.VMEM((members, points, points), jnp.bfloat16),
            pltpu.VMEM((levels, points, rank), jnp.bfloat16),
            pltpu.VMEM((levels, columns, rank), jnp.float32),
            arrived,
            pltpu.VMEM((levels, columns, rank), jnp.bfloat16),
            pltpu.VMEM((points, columns), jnp.float32),
            pltpu.SemaphoreType.DMA((4,)),
            pltpu.SemaphoreType.DMA,
            pltpu.SemaphoreType.DMA((levels,)),
            pltpu.SemaphoreType.DMA((levels,)),
            pltpu.SemaphoreType.DMA((levels,)),
            pltpu.SemaphoreType.DMA((levels,)),
            pltpu.SemaphoreType.DMA((2,)),
            pltpu.SemaphoreType.DMA((2,)),
        ],
        compiler_params=pltpu.CompilerParams(
            collective_id=0, has_side_effects=True, vmem_limit_bytes=60 * 2**20
        ),
        cost_estimate=pl.CostEstimate(flops=flops, bytes_accessed=2 * near_blocks.size, transcendentals=0),
    )(near_offsets, probes, near_blocks, far_basis)


def swapped(value, axis, bit):
    mask = 2**bit
    pairs = [(source, source ^ mask) for source in range(lax.axis_size(axis))]
    return lax.ppermute(value, axis, pairs)


def upper(output, probes, far_basis, first):
    levels = far_basis.shape[0]
    partial_sums = {
        level: lax.dot_general(
            far_basis[level], probes, (((0,), (0,)), ((), ())), preferred_element_type=jnp.float32
        )
        for level in range(first, levels)
    }
    leaf_bits = lax.axis_size("leaf").bit_length() - 1
    for bit in range(levels):
        axis, axis_bit = ("leaf", bit) if bit < leaf_bits else ("slab", bit - leaf_bits)
        kept = [level for level in range(first, levels) if level >= bit]
        incoming = swapped(jnp.stack([partial_sums[level] for level in kept]), axis, axis_bit)
        for place, level in enumerate(kept):
            if level == bit:
                coupling = (incoming[place] * 2.0 ** (-0.5 * level)).astype(jnp.bfloat16)
                output = output + jnp.dot(
                    far_basis[level], coupling, preferred_element_type=jnp.float32
                )
            else:
                partial_sums[level] = partial_sums[level] + incoming[place]
    return output


def body(probes, near_blocks, near_offsets, far_basis):
    levels = far_basis.shape[0]
    first = min(levels, DIRECT_LEVELS)
    near_sum, coupling = direct(probes, near_blocks, near_offsets, far_basis, first)
    output = near_sum + jnp.einsum(
        "lpr,lqr->pq", far_basis[:first], coupling, preferred_element_type=jnp.float32
    )
    if levels > first:
        output = upper(output, probes, far_basis, first)
    return output


def solution(mesh):
    return jax.shard_map(
        body,
        mesh=mesh,
        in_specs=(
            P(("slab", "leaf"), None),
            P(("slab", "leaf"), None, None, None),
            P(("slab", "leaf"), None),
            P(None, ("slab", "leaf"), None),
        ),
        out_specs=P(("slab", "leaf"), None),
        check_vma=False,
    )
```

```python
import functools

import jax
import jax.numpy as jnp
from jax import lax
from jax.experimental import pallas as pl
from jax.experimental.pallas import tpu as pltpu
from jax.sharding import PartitionSpec as P

MESH = pl.DeviceIdType.MESH
DIRECT_LEVELS = 5


def flipped(index, mask):
    bit = 1
    result = index
    while bit <= mask:
        if mask & bit:
            result = result + bit * (1 - 2 * ((index // bit) % 2))
        bit *= 2
    return result


def kernel(
    levels, slabs, leaves, offsets_hbm, probes_hbm, near_hbm, far_hbm, out_hbm, coupling,
    offsets, window, near, far, partial, paired, arrived, piece, out,
    load_sem, out_sem, pair_send, pair_recv, relay_send, relay_recv,
    sum_send, sum_recv, piece_send, piece_recv, probe_send, probe_recv,
):
    slab, leaf = lax.axis_index("slab"), lax.axis_index("leaf")
    me = slab * leaves + leaf
    core = leaf % 2
    total = slabs * leaves
    group = 2**levels
    columns = partial.shape[1]

    def device(mask):
        return flipped(slab, mask // leaves), flipped(leaf, mask % leaves)

    def along(step):
        other = me + step
        return other // leaves, other % leaves

    load_probes = pltpu.make_async_copy(probes_hbm, window.at[1], load_sem.at[0])
    load_far = pltpu.make_async_copy(far_hbm.at[pl.ds(0, levels)], far, load_sem.at[1])
    load_near = pltpu.make_async_copy(near_hbm.at[0], near, load_sem.at[2])
    load_offsets = pltpu.make_async_copy(offsets_hbm, offsets, load_sem.at[3])
    load_probes.start()
    load_far.start()
    load_offsets.start()
    load_near.start()

    has_low, has_high = me > 0, me < total - 1
    barrier = pltpu.get_barrier_semaphore()
    for mask in [1] + list(range(2, group, 2)):
        pl.semaphore_signal(barrier, inc=1, device_id=device(mask), device_id_type=MESH)
    beside = jnp.where(core == 0, me > 0, me < total - 1)

    @pl.when(beside)
    def _():
        pl.semaphore_signal(barrier, inc=1, device_id=along(2 * core - 1), device_id_type=MESH)

    load_probes.wait()
    load_far.wait()
    turned = window[1].T
    for level in reversed(range(levels)):
        partial[level] = jnp.dot(turned, far[level], preferred_element_type=jnp.float32)
    piece[0] = partial[0].astype(jnp.bfloat16)

    pl.semaphore_wait(barrier, group // 2 + beside.astype(jnp.int32))

    def remote(source, target, send, recv, where):
        return pltpu.make_async_remote_copy(
            src_ref=source, dst_ref=target, send_sem=send, recv_sem=recv,
            device_id=where, device_id_type=MESH,
        )

    def height_of(level):
        return columns // 2 ** (level - 1)

    def rows_of(level, index):
        height = height_of(level)
        return pl.ds(pl.multiple_of((index % 2**level) // 2 * height, height), height)

    def await_bytes(ref, sem):
        pltpu.make_async_copy(ref, ref, sem).wait()

    def on_core(action):
        for side in range(2):
            owned = [level for level in reversed(range(1, levels)) if level % 2 == side]
            others = [level for level in reversed(range(1, levels)) if level % 2 != side]
            pl.when(core == side)(functools.partial(action, owned, others))

    def hand_over(owned, others):
        for level in others:
            remote(
                partial.at[level], paired.at[level],
                pair_send.at[level], pair_recv.at[level], device(1),
            ).start()

    on_core(hand_over)
    remote(piece.at[0], coupling.at[0], piece_send.at[0], piece_recv.at[0], device(1)).start()
    to_low = remote(window.at[1], window.at[2], probe_send.at[0], probe_recv.at[1], along(-1))
    to_high = remote(window.at[1], window.at[0], probe_send.at[1], probe_recv.at[0], along(1))
    pl.when(has_low)(to_low.start)
    pl.when(has_high)(to_high.start)

    def announce(level, value):
        rows = pl.ds(0, height_of(level))
        piece[level, rows] = (value * 2.0 ** (-0.5 * level)).astype(jnp.bfloat16)
        for mask in reversed(range(2**level, 2 ** (level + 1), 2)):
            remote(
                piece.at[level, rows], coupling.at[level, rows_of(level, me)],
                piece_send.at[level], piece_recv.at[level], device(mask),
            ).start()

    def reduce(owned, others):
        for level in owned:
            await_bytes(paired.at[level], pair_recv.at[level])
            value = partial[level] + paired[level]
            if level == 1:
                announce(level, value)
                continue
            partial[level] = value
            for mask in reversed(range(2, 2**level, 2)):
                remote(
                    partial.at[level, rows_of(level, flipped(me, mask))],
                    arrived[level - 2].at[mask // 2],
                    sum_send.at[level], sum_recv.at[level], device(mask),
                ).start()
        for level in owned:
            if level == 1:
                continue
            chips = 2 ** (level - 1)
            await_bytes(arrived[level - 2].at[pl.ds(1, chips - 1)], sum_recv.at[level])
            value = partial[level, rows_of(level, me)]
            for chip in range(1, chips):
                value = value + arrived[level - 2][chip]
            announce(level, value)

    on_core(reduce)

    @pl.when(jnp.logical_not(has_low))
    def _():
        window[0] = jnp.zeros_like(window[0])

    @pl.when(jnp.logical_not(has_high))
    def _():
        window[2] = jnp.zeros_like(window[2])

    pl.when(has_high)(lambda: await_bytes(window.at[2], probe_recv.at[1]))
    pl.when(has_low)(lambda: await_bytes(window.at[0], probe_recv.at[0]))
    load_near.wait()
    load_offsets.wait()
    members = near.shape[0]
    value = jnp.dot(near[0], window[offsets[0, 0] + 1], preferred_element_type=jnp.float32)
    for member in range(1, members):
        value = value + jnp.dot(
            near[member], window[offsets[0, member] + 1], preferred_element_type=jnp.float32
        )
    out[...] = value

    store = pltpu.make_async_copy(out, out_hbm, out_sem)
    store.start()

    def relay(owned, others):
        for level in reversed(owned):
            await_bytes(coupling.at[level], piece_recv.at[level])
            remote(
                coupling.at[level], coupling.at[level],
                relay_send.at[level], relay_recv.at[level], device(1),
            ).start()
        await_bytes(coupling.at[0], piece_recv.at[0])
        for level in others:
            await_bytes(partial.at[level], pair_send.at[level])
            await_bytes(coupling.at[level], relay_recv.at[level])
        for level in owned:
            if level > 1:
                await_bytes(partial.at[level, pl.ds(0, columns - height_of(level))], sum_send.at[level])
            await_bytes(coupling.at[level], piece_send.at[level])
            await_bytes(coupling.at[level], relay_send.at[level])

    on_core(relay)
    await_bytes(piece.at[0], piece_send.at[0])
    pl.when(has_low)(to_low.wait_send)
    pl.when(has_high)(to_high.wait_send)
    store.wait()


def direct(probes, near_blocks, near_offsets, far_basis, levels):
    points, columns = probes.shape
    rank = far_basis.shape[2]
    members = near_blocks.shape[1]
    slabs, leaves = lax.axis_size("slab"), lax.axis_size("leaf")
    arrived = [
        pltpu.VMEM((2 ** (level - 1), columns // 2 ** (level - 1), rank), jnp.float32)
        for level in range(2, levels)
    ]
    flops = 2 * points * columns * (members * points + 2 * levels * rank)
    return pl.pallas_call(
        functools.partial(kernel, levels, slabs, leaves),
        out_shape=[
            jax.ShapeDtypeStruct((points, columns), jnp.float32),
            jax.ShapeDtypeStruct((levels, columns, rank), jnp.bfloat16),
        ],
        in_specs=[pl.BlockSpec(memory_space=pl.ANY)] * 4,
        out_specs=[pl.BlockSpec(memory_space=pl.ANY)] * 2,
        scratch_shapes=[
            pltpu.SMEM((1, members), jnp.int32),
            pltpu.VMEM((3, points, columns), jnp.bfloat16),
            pltpu.VMEM((members, points, points), jnp.bfloat16),
            pltpu.VMEM((levels, points, rank), jnp.bfloat16),
            pltpu.VMEM((levels, columns, rank), jnp.float32),
            pltpu.VMEM((levels, columns, rank), jnp.float32),
            arrived,
            pltpu.VMEM((levels, columns, rank), jnp.bfloat16),
            pltpu.VMEM((points, columns), jnp.float32),
            pltpu.SemaphoreType.DMA((4,)),
            pltpu.SemaphoreType.DMA,
            pltpu.SemaphoreType.DMA((levels,)),
            pltpu.SemaphoreType.DMA((levels,)),
            pltpu.SemaphoreType.DMA((levels,)),
            pltpu.SemaphoreType.DMA((levels,)),
            pltpu.SemaphoreType.DMA((levels,)),
            pltpu.SemaphoreType.DMA((levels,)),
            pltpu.SemaphoreType.DMA((levels,)),
            pltpu.SemaphoreType.DMA((levels,)),
            pltpu.SemaphoreType.DMA((2,)),
            pltpu.SemaphoreType.DMA((2,)),
        ],
        compiler_params=pltpu.CompilerParams(
            collective_id=0, has_side_effects=True, vmem_limit_bytes=60 * 2**20
        ),
        cost_estimate=pl.CostEstimate(flops=flops, bytes_accessed=2 * near_blocks.size, transcendentals=0),
    )(near_offsets, probes, near_blocks, far_basis)


def swapped(value, axis, bit):
    mask = 2**bit
    pairs = [(source, source ^ mask) for source in range(lax.axis_size(axis))]
    return lax.ppermute(value, axis, pairs)


def upper(output, probes, far_basis, first):
    levels = far_basis.shape[0]
    partial_sums = {
        level: lax.dot_general(
            far_basis[level], probes, (((0,), (0,)), ((), ())), preferred_element_type=jnp.float32
        )
        for level in range(first, levels)
    }
    leaf_bits = lax.axis_size("leaf").bit_length() - 1
    for bit in range(levels):
        axis, axis_bit = ("leaf", bit) if bit < leaf_bits else ("slab", bit - leaf_bits)
        kept = [level for level in range(first, levels) if level >= bit]
        incoming = swapped(jnp.stack([partial_sums[level] for level in kept]), axis, axis_bit)
        for place, level in enumerate(kept):
            if level == bit:
                coupling = (incoming[place] * 2.0 ** (-0.5 * level)).astype(jnp.bfloat16)
                output = output + jnp.dot(
                    far_basis[level], coupling, preferred_element_type=jnp.float32
                )
            else:
                partial_sums[level] = partial_sums[level] + incoming[place]
    return output


def body(probes, near_blocks, near_offsets, far_basis):
    levels = far_basis.shape[0]
    first = min(levels, DIRECT_LEVELS)
    near_sum, coupling = direct(probes, near_blocks, near_offsets, far_basis, first)
    output = near_sum
    for level in range(first):
        output = output + lax.dot_general(
            far_basis[level], coupling[level], (((1,), (1,)), ((), ())),
            preferred_element_type=jnp.float32,
        )
    if levels > first:
        output = upper(output, probes, far_basis, first)
    return output


def solution(mesh):
    return jax.shard_map(
        body,
        mesh=mesh,
        in_specs=(
            P(("slab", "leaf"), None),
            P(("slab", "leaf"), None, None, None),
            P(("slab", "leaf"), None),
            P(None, ("slab", "leaf"), None),
        ),
        out_specs=P(("slab", "leaf"), None),
        check_vma=False,
    )
```

```python
import functools

import jax
import jax.numpy as jnp
from jax import lax
from jax.experimental import pallas as pl
from jax.experimental.pallas import tpu as pltpu
from jax.sharding import PartitionSpec as P

MESH = pl.DeviceIdType.MESH
DIRECT_LEVELS = 5


def flipped(index, mask):
    bit = 1
    result = index
    while bit <= mask:
        if mask & bit:
            result = result + bit * (1 - 2 * ((index // bit) % 2))
        bit *= 2
    return result


def owner_parity(level):
    return None if level < 3 else level % 2


def owner_count(level):
    return 2**level if level < 3 else 2 ** (level - 1)


def kernel(
    levels, slabs, leaves, offsets_hbm, probes_hbm, near_hbm, far_hbm, out_hbm, coupling,
    offsets, window, near, far, partial, arrived, piece, out,
    load_sem, out_sem, sum_send, sum_recv, piece_send, piece_recv, probe_send, probe_recv,
):
    slab, leaf = lax.axis_index("slab"), lax.axis_index("leaf")
    me = slab * leaves + leaf
    core = leaf % 2
    total = slabs * leaves
    group = 2**levels
    rank = partial.shape[1]
    points = window.shape[1]

    def device(mask):
        return flipped(slab, mask // leaves), flipped(leaf, mask % leaves)

    def along(step):
        other = me + step
        return other // leaves, other % leaves

    load_probes = pltpu.make_async_copy(probes_hbm, window.at[1], load_sem.at[0])
    load_far = pltpu.make_async_copy(far_hbm.at[pl.ds(0, levels)], far, load_sem.at[1])
    load_near = pltpu.make_async_copy(near_hbm.at[0], near, load_sem.at[2])
    load_offsets = pltpu.make_async_copy(offsets_hbm, offsets, load_sem.at[3])
    load_probes.start()
    load_far.start()
    load_offsets.start()
    load_near.start()

    has_low, has_high = me > 0, me < total - 1
    barrier = pltpu.get_barrier_semaphore()
    for mask in range(1, group):
        pl.semaphore_signal(barrier, inc=1, device_id=device(mask), device_id_type=MESH)
    if total > group:
        low_outside = jnp.logical_and(has_low, me % group == 0)
        high_outside = jnp.logical_and(has_high, me % group == group - 1)
        for outside, step in ((low_outside, -1), (high_outside, 1)):
            @pl.when(outside)
            def _():
                pl.semaphore_signal(barrier, inc=1, device_id=along(step), device_id_type=MESH)

    load_probes.wait()
    load_far.wait()
    turned = window[1].T
    for level in reversed(range(levels)):
        partial[level] = jnp.dot(turned, far[level], preferred_element_type=jnp.float32)
    piece[0] = partial[0].astype(jnp.bfloat16)

    pl.semaphore_wait(barrier, group - 1)
    if total > group:
        for outside in (low_outside, high_outside):
            @pl.when(outside)
            def _():
                pl.semaphore_wait(barrier, 1)

    def remote(source, target, send, recv, where):
        return pltpu.make_async_remote_copy(
            src_ref=source, dst_ref=target, send_sem=send, recv_sem=recv,
            device_id=where, device_id_type=MESH,
        )

    def rows_of(level, index):
        count = owner_count(level)
        chunk = index % 2**level
        if owner_parity(level) is not None:
            chunk = chunk // 2
        height = rank // count
        return pl.ds(pl.multiple_of(chunk * height, height), height)

    to_low = remote(window.at[1], window.at[2], probe_send.at[0], probe_recv.at[1], along(-1))
    to_high = remote(window.at[1], window.at[0], probe_send.at[1], probe_recv.at[0], along(1))
    pl.when(has_low)(to_low.start)
    pl.when(has_high)(to_high.start)

    for level in reversed(range(1, levels)):
        parity = owner_parity(level)
        if parity is None:
            for mask in range(1, 2**level):
                where = device(mask)
                remote(
                    partial.at[level, rows_of(level, flipped(me, mask))],
                    arrived[level - 1].at[mask],
                    sum_send.at[level], sum_recv.at[level], where,
                ).start()
        else:
            differs = (core + parity) % 2
            for pair in reversed(range(2 ** (level - 1))):
                where_slab, where_leaf = device(2 * pair)
                where = where_slab, where_leaf - core + parity
                index = where[0] * leaves + where[1]

                def send():
                    remote(
                        partial.at[level, rows_of(level, index)],
                        arrived[level - 1].at[2 * pair + differs],
                        sum_send.at[level], sum_recv.at[level], where,
                    ).start()

                if pair == 0:
                    pl.when(differs == 1)(send)
                else:
                    send()

    remote(piece.at[0], coupling.at[0], piece_send.at[0], piece_recv.at[0], device(1)).start()

    def await_bytes(ref, sem):
        pltpu.make_async_copy(ref, ref, sem).wait()

    def finish(level):
        rows = rows_of(level, me)
        height = rank // owner_count(level)
        members = 2**level
        await_bytes(arrived[level - 1].at[pl.ds(1, members - 1)], sum_recv.at[level])
        value = partial[level, rows]
        for member in range(1, members):
            value = value + arrived[level - 1][member]
        value = (value * 2.0 ** (-0.5 * level)).astype(jnp.bfloat16)
        piece[level, pl.ds(0, height)] = value
        for mask in reversed(range(members, 2 * members)):
            remote(
                piece.at[level, pl.ds(0, height)], coupling.at[level, rows],
                piece_send.at[level], piece_recv.at[level], device(mask),
            ).start()

    for level in reversed(range(1, levels)):
        parity = owner_parity(level)
        if parity is None:
            finish(level)
        else:
            pl.when(core == parity)(functools.partial(finish, level))

    @pl.when(jnp.logical_not(has_low))
    def _():
        window[0] = jnp.zeros_like(window[0])

    @pl.when(jnp.logical_not(has_high))
    def _():
        window[2] = jnp.zeros_like(window[2])

    pl.when(has_high)(lambda: await_bytes(window.at[2], probe_recv.at[1]))
    pl.when(has_low)(lambda: await_bytes(window.at[0], probe_recv.at[0]))
    load_near.wait()
    load_offsets.wait()
    members = near.shape[0]
    value = jnp.dot(near[0], window[offsets[0, 0] + 1], preferred_element_type=jnp.float32)
    for member in range(1, members):
        value = value + jnp.dot(
            near[member], window[offsets[0, member] + 1], preferred_element_type=jnp.float32
        )
    out[...] = value

    store = pltpu.make_async_copy(out, out_hbm, out_sem)
    store.start()
    for level in range(levels):
        await_bytes(coupling.at[level], piece_recv.at[level])

    await_bytes(piece.at[0], piece_send.at[0])
    for level in range(1, levels):
        parity = owner_parity(level)
        height = rank // owner_count(level)
        if parity is None:
            await_bytes(partial.at[level, pl.ds(0, rank - height)], sum_send.at[level])
            await_bytes(coupling.at[level], piece_send.at[level])
        else:
            @pl.when(core == parity)
            def _():
                await_bytes(partial.at[level, pl.ds(0, rank - height)], sum_send.at[level])
                await_bytes(coupling.at[pl.ds(0, 2)], piece_send.at[level])

            @pl.when(core != parity)
            def _():
                await_bytes(partial.at[level], sum_send.at[level])

    pl.when(has_low)(to_low.wait_send)
    pl.when(has_high)(to_high.wait_send)
    store.wait()


def direct(probes, near_blocks, near_offsets, far_basis, levels):
    points, columns = probes.shape
    rank = far_basis.shape[2]
    members = near_blocks.shape[1]
    slabs, leaves = lax.axis_size("slab"), lax.axis_size("leaf")
    arrived = [
        pltpu.VMEM((2**level, rank // owner_count(level), columns), jnp.float32)
        for level in range(1, levels)
    ]
    flops = 2 * points * columns * (members * points + 2 * levels * rank)
    return pl.pallas_call(
        functools.partial(kernel, levels, slabs, leaves),
        out_shape=[
            jax.ShapeDtypeStruct((points, columns), jnp.float32),
            jax.ShapeDtypeStruct((levels, columns, rank), jnp.bfloat16),
        ],
        in_specs=[pl.BlockSpec(memory_space=pl.ANY)] * 4,
        out_specs=[pl.BlockSpec(memory_space=pl.ANY)] * 2,
        scratch_shapes=[
            pltpu.SMEM((1, members), jnp.int32),
            pltpu.VMEM((3, points, columns), jnp.bfloat16),
            pltpu.VMEM((members, points, points), jnp.bfloat16),
            pltpu.VMEM((levels, points, rank), jnp.bfloat16),
            pltpu.VMEM((levels, columns, rank), jnp.float32),
            arrived,
            pltpu.VMEM((levels, columns, rank), jnp.bfloat16),
            pltpu.VMEM((points, columns), jnp.float32),
            pltpu.SemaphoreType.DMA((4,)),
            pltpu.SemaphoreType.DMA,
            pltpu.SemaphoreType.DMA((levels,)),
            pltpu.SemaphoreType.DMA((levels,)),
            pltpu.SemaphoreType.DMA((levels,)),
            pltpu.SemaphoreType.DMA((levels,)),
            pltpu.SemaphoreType.DMA((2,)),
            pltpu.SemaphoreType.DMA((2,)),
        ],
        compiler_params=pltpu.CompilerParams(
            collective_id=0, has_side_effects=True, vmem_limit_bytes=60 * 2**20
        ),
        cost_estimate=pl.CostEstimate(flops=flops, bytes_accessed=2 * near_blocks.size, transcendentals=0),
    )(near_offsets, probes, near_blocks, far_basis)


def swapped(value, axis, bit):
    mask = 2**bit
    pairs = [(source, source ^ mask) for source in range(lax.axis_size(axis))]
    return lax.ppermute(value, axis, pairs)


def upper(output, probes, far_basis, first):
    levels = far_basis.shape[0]
    partial_sums = {
        level: lax.dot_general(
            far_basis[level], probes, (((0,), (0,)), ((), ())), preferred_element_type=jnp.float32
        )
        for level in range(first, levels)
    }
    leaf_bits = lax.axis_size("leaf").bit_length() - 1
    for bit in range(levels):
        axis, axis_bit = ("leaf", bit) if bit < leaf_bits else ("slab", bit - leaf_bits)
        kept = [level for level in range(first, levels) if level >= bit]
        incoming = swapped(jnp.stack([partial_sums[level] for level in kept]), axis, axis_bit)
        for place, level in enumerate(kept):
            if level == bit:
                coupling = (incoming[place] * 2.0 ** (-0.5 * level)).astype(jnp.bfloat16)
                output = output + jnp.dot(
                    far_basis[level], coupling, preferred_element_type=jnp.float32
                )
            else:
                partial_sums[level] = partial_sums[level] + incoming[place]
    return output


def body(probes, near_blocks, near_offsets, far_basis):
    levels = far_basis.shape[0]
    first = min(levels, DIRECT_LEVELS)
    near_sum, coupling = direct(probes, near_blocks, near_offsets, far_basis, first)
    output = near_sum + jnp.einsum(
        "lpr,lqr->pq", far_basis[:first], coupling, preferred_element_type=jnp.float32
    )
    if levels > first:
        output = upper(output, probes, far_basis, first)
    return output


def solution(mesh):
    return jax.shard_map(
        body,
        mesh=mesh,
        in_specs=(
            P(("slab", "leaf"), None),
            P(("slab", "leaf"), None, None, None),
            P(("slab", "leaf"), None),
            P(None, ("slab", "leaf"), None),
        ),
        out_specs=P(("slab", "leaf"), None),
        check_vma=False,
    )
```

```python
import functools

import jax
import jax.numpy as jnp
from jax import lax
from jax.experimental import pallas as pl
from jax.experimental.pallas import tpu as pltpu
from jax.sharding import PartitionSpec as P

MESH = pl.DeviceIdType.MESH
DIRECT_LEVELS = 5


def flipped(index, mask):
    bit = 1
    result = index
    while bit <= mask:
        if mask & bit:
            result = result + bit * (1 - 2 * ((index // bit) % 2))
        bit *= 2
    return result


def owner_parity(level):
    return None if level < 3 else level % 2


def owner_count(level):
    return 2**level if level < 3 else 2 ** (level - 1)


def kernel(
    levels, slabs, leaves, offsets_hbm, probes_hbm, near_hbm, far_hbm, out_hbm, coupling,
    offsets, window, near, far, partial, arrived, piece, out,
    load_sem, out_sem, sum_send, sum_recv, piece_send, piece_recv, probe_send, probe_recv,
):
    slab, leaf = lax.axis_index("slab"), lax.axis_index("leaf")
    me = slab * leaves + leaf
    core = leaf % 2
    total = slabs * leaves
    group = 2**levels
    rank = partial.shape[1]
    points = window.shape[1]

    def device(mask):
        return flipped(slab, mask // leaves), flipped(leaf, mask % leaves)

    def along(step):
        other = me + step
        return other // leaves, other % leaves

    load_probes = pltpu.make_async_copy(probes_hbm, window.at[1], load_sem.at[0])
    load_far = pltpu.make_async_copy(far_hbm.at[pl.ds(0, levels)], far, load_sem.at[1])
    load_near = pltpu.make_async_copy(near_hbm.at[0], near, load_sem.at[2])
    load_offsets = pltpu.make_async_copy(offsets_hbm, offsets, load_sem.at[3])
    load_probes.start()
    load_far.start()
    load_offsets.start()
    load_near.start()

    has_low, has_high = me > 0, me < total - 1
    barrier = pltpu.get_barrier_semaphore()
    for mask in range(1, group):
        pl.semaphore_signal(barrier, inc=1, device_id=device(mask), device_id_type=MESH)
    if total > group:
        low_outside = jnp.logical_and(has_low, me % group == 0)
        high_outside = jnp.logical_and(has_high, me % group == group - 1)
        for outside, step in ((low_outside, -1), (high_outside, 1)):
            @pl.when(outside)
            def _():
                pl.semaphore_signal(barrier, inc=1, device_id=along(step), device_id_type=MESH)

    load_probes.wait()
    load_far.wait()
    turned = window[1].T
    for level in reversed(range(levels)):
        partial[level] = jnp.dot(turned, far[level], preferred_element_type=jnp.float32)
    piece[0] = partial[0].astype(jnp.bfloat16)

    pl.semaphore_wait(barrier, group - 1)
    if total > group:
        for outside in (low_outside, high_outside):
            @pl.when(outside)
            def _():
                pl.semaphore_wait(barrier, 1)

    def remote(source, target, send, recv, where):
        return pltpu.make_async_remote_copy(
            src_ref=source, dst_ref=target, send_sem=send, recv_sem=recv,
            device_id=where, device_id_type=MESH,
        )

    def rows_of(level, index):
        count = owner_count(level)
        chunk = index % 2**level
        if owner_parity(level) is not None:
            chunk = chunk // 2
        height = rank // count
        return pl.ds(pl.multiple_of(chunk * height, height), height)

    for level in reversed(range(1, levels)):
        parity = owner_parity(level)
        if parity is None:
            for mask in range(1, 2**level):
                where = device(mask)
                remote(
                    partial.at[level, rows_of(level, flipped(me, mask))],
                    arrived[level - 1].at[mask],
                    sum_send.at[level], sum_recv.at[level], where,
                ).start()
        else:
            differs = (core + parity) % 2
            for pair in reversed(range(2 ** (level - 1))):
                where_slab, where_leaf = device(2 * pair)
                where = where_slab, where_leaf - core + parity
                index = where[0] * leaves + where[1]

                def send():
                    remote(
                        partial.at[level, rows_of(level, index)],
                        arrived[level - 1].at[2 * pair + differs],
                        sum_send.at[level], sum_recv.at[level], where,
                    ).start()

                if pair == 0:
                    pl.when(differs == 1)(send)
                else:
                    send()

    remote(piece.at[0], coupling.at[0], piece_send.at[0], piece_recv.at[0], device(1)).start()

    to_low = remote(window.at[1], window.at[2], probe_send.at[0], probe_recv.at[1], along(-1))
    to_high = remote(window.at[1], window.at[0], probe_send.at[1], probe_recv.at[0], along(1))
    pl.when(has_low)(to_low.start)
    pl.when(has_high)(to_high.start)

    def await_bytes(ref, sem):
        pltpu.make_async_copy(ref, ref, sem).wait()

    def finish(level):
        rows = rows_of(level, me)
        height = rank // owner_count(level)
        members = 2**level
        await_bytes(arrived[level - 1].at[pl.ds(1, members - 1)], sum_recv.at[level])
        value = partial[level, rows]
        for member in range(1, members):
            value = value + arrived[level - 1][member]
        value = (value * 2.0 ** (-0.5 * level)).astype(jnp.bfloat16)
        piece[level, pl.ds(0, height)] = value
        for mask in reversed(range(members, 2 * members)):
            remote(
                piece.at[level, pl.ds(0, height)], coupling.at[level, rows],
                piece_send.at[level], piece_recv.at[level], device(mask),
            ).start()

    for level in range(1, levels):
        parity = owner_parity(level)
        if parity is None:
            finish(level)
        else:
            pl.when(core == parity)(functools.partial(finish, level))

    @pl.when(jnp.logical_not(has_low))
    def _():
        window[0] = jnp.zeros_like(window[0])

    @pl.when(jnp.logical_not(has_high))
    def _():
        window[2] = jnp.zeros_like(window[2])

    pl.when(has_high)(lambda: await_bytes(window.at[2], probe_recv.at[1]))
    pl.when(has_low)(lambda: await_bytes(window.at[0], probe_recv.at[0]))
    load_near.wait()
    load_offsets.wait()
    members = near.shape[0]
    value = jnp.dot(near[0], window[offsets[0, 0] + 1], preferred_element_type=jnp.float32)
    for member in range(1, members):
        value = value + jnp.dot(
            near[member], window[offsets[0, member] + 1], preferred_element_type=jnp.float32
        )
    out[...] = value

    store = pltpu.make_async_copy(out, out_hbm, out_sem)
    store.start()
    for level in range(levels):
        await_bytes(coupling.at[level], piece_recv.at[level])

    await_bytes(piece.at[0], piece_send.at[0])
    for level in range(1, levels):
        parity = owner_parity(level)
        height = rank // owner_count(level)
        if parity is None:
            await_bytes(partial.at[level, pl.ds(0, rank - height)], sum_send.at[level])
            await_bytes(coupling.at[level], piece_send.at[level])
        else:
            @pl.when(core == parity)
            def _():
                await_bytes(partial.at[level, pl.ds(0, rank - height)], sum_send.at[level])
                await_bytes(coupling.at[pl.ds(0, 2)], piece_send.at[level])

            @pl.when(core != parity)
            def _():
                await_bytes(partial.at[level], sum_send.at[level])

    pl.when(has_low)(to_low.wait_send)
    pl.when(has_high)(to_high.wait_send)
    store.wait()


def direct(probes, near_blocks, near_offsets, far_basis, levels):
    points, columns = probes.shape
    rank = far_basis.shape[2]
    members = near_blocks.shape[1]
    slabs, leaves = lax.axis_size("slab"), lax.axis_size("leaf")
    arrived = [
        pltpu.VMEM((2**level, rank // owner_count(level), columns), jnp.float32)
        for level in range(1, levels)
    ]
    flops = 2 * points * columns * (members * points + 2 * levels * rank)
    return pl.pallas_call(
        functools.partial(kernel, levels, slabs, leaves),
        out_shape=[
            jax.ShapeDtypeStruct((points, columns), jnp.float32),
            jax.ShapeDtypeStruct((levels, columns, rank), jnp.bfloat16),
        ],
        in_specs=[pl.BlockSpec(memory_space=pl.ANY)] * 4,
        out_specs=[pl.BlockSpec(memory_space=pl.ANY)] * 2,
        scratch_shapes=[
            pltpu.SMEM((1, members), jnp.int32),
            pltpu.VMEM((3, points, columns), jnp.bfloat16),
            pltpu.VMEM((members, points, points), jnp.bfloat16),
            pltpu.VMEM((levels, points, rank), jnp.bfloat16),
            pltpu.VMEM((levels, columns, rank), jnp.float32),
            arrived,
            pltpu.VMEM((levels, columns, rank), jnp.bfloat16),
            pltpu.VMEM((points, columns), jnp.float32),
            pltpu.SemaphoreType.DMA((4,)),
            pltpu.SemaphoreType.DMA,
            pltpu.SemaphoreType.DMA((levels,)),
            pltpu.SemaphoreType.DMA((levels,)),
            pltpu.SemaphoreType.DMA((levels,)),
            pltpu.SemaphoreType.DMA((levels,)),
            pltpu.SemaphoreType.DMA((2,)),
            pltpu.SemaphoreType.DMA((2,)),
        ],
        compiler_params=pltpu.CompilerParams(
            collective_id=0, has_side_effects=True, vmem_limit_bytes=60 * 2**20
        ),
        cost_estimate=pl.CostEstimate(flops=flops, bytes_accessed=2 * near_blocks.size, transcendentals=0),
    )(near_offsets, probes, near_blocks, far_basis)


def swapped(value, axis, bit):
    mask = 2**bit
    pairs = [(source, source ^ mask) for source in range(lax.axis_size(axis))]
    return lax.ppermute(value, axis, pairs)


def upper(output, probes, far_basis, first):
    levels = far_basis.shape[0]
    partial_sums = {
        level: lax.dot_general(
            far_basis[level], probes, (((0,), (0,)), ((), ())), preferred_element_type=jnp.float32
        )
        for level in range(first, levels)
    }
    leaf_bits = lax.axis_size("leaf").bit_length() - 1
    for bit in range(levels):
        axis, axis_bit = ("leaf", bit) if bit < leaf_bits else ("slab", bit - leaf_bits)
        kept = [level for level in range(first, levels) if level >= bit]
        incoming = swapped(jnp.stack([partial_sums[level] for level in kept]), axis, axis_bit)
        for place, level in enumerate(kept):
            if level == bit:
                coupling = (incoming[place] * 2.0 ** (-0.5 * level)).astype(jnp.bfloat16)
                output = output + jnp.dot(
                    far_basis[level], coupling, preferred_element_type=jnp.float32
                )
            else:
                partial_sums[level] = partial_sums[level] + incoming[place]
    return output


def body(probes, near_blocks, near_offsets, far_basis):
    levels = far_basis.shape[0]
    first = min(levels, DIRECT_LEVELS)
    near_sum, coupling = direct(probes, near_blocks, near_offsets, far_basis, first)
    output = near_sum + jnp.einsum(
        "lpr,lqr->pq", far_basis[:first], coupling, preferred_element_type=jnp.float32
    )
    if levels > first:
        output = upper(output, probes, far_basis, first)
    return output


def solution(mesh):
    return jax.shard_map(
        body,
        mesh=mesh,
        in_specs=(
            P(("slab", "leaf"), None),
            P(("slab", "leaf"), None, None, None),
            P(("slab", "leaf"), None),
            P(None, ("slab", "leaf"), None),
        ),
        out_specs=P(("slab", "leaf"), None),
        check_vma=False,
    )
```
